1024 devices in a mesh: head: 8 (over x, z_hi), seq: 128 (over z_lo, y, core).
Axes of the slice: x: 4, y: 8, z: 16 (z_hi: 2, z_lo: 8; z = z_hi * 8 + z_lo), core: 2. Of those that a mesh axis runs over, the one named last changes fastest.
Arguments:
- queries: bfloat16 [128, 128, 576], P('seq', 'head'), may hold values from -400 to 400
- query_pos: int32 [128], replicated, may hold values from 32259 to 32767, as said below
- latents: bfloat16 [32768, 576], P('seq'), may hold values from -6 to 6
- valid_keys: int32 [128], P('seq'), may hold values from 128 to 256, as said below
- output_gradient: bfloat16 [128, 128, 512], P('seq', 'head'), may hold values from -600 to 600
- kv_down: bfloat16 [7168, 576], P('head'), may hold values from -0.0625 to 0.0625
Outputs:
- latent_grad: float32 [32768, 576], P('seq')
- input_grad: bfloat16 [32768, 7168], P('seq', 'head')
The draws below stay inside these ranges and needn't reach their ends.
Inputs may be any that keep to these rules, and one draw needn't show every extreme that they name: `query_pos`: positions rise strictly with the query index, consecutive ones differ by 1 to 4, and the last is 32767. The first valid_keys[s] positions of shard s are valid; some shard is full and some holds exactly half.
All inputs are finite; a program needn't handle non-finite values.
Results may differ from the reference program's by a relative error of at most 0.015.
Values may be sent and summed in bfloat16 or wider, within the bound.
A program may use at most 32 MiB of HBM per device.

```python
import jax
import jax.numpy as jnp
from jax import lax

D = 7168
LATENT_WIDTH = 512
HEADS_DEV = 16
SHARD_KEY_COUNT = 256
LAT = 576
HEAD_TOTAL = 128
S = 32768
QUERY_TOTAL = 128


def sign_pattern(key):
    raw = jax.random.normal(jax.random.fold_in(key, 31), (LAT,), jnp.float32)
    return jnp.where(raw > 0.0, 2.0, -2.0)


def shared_latents(key):
    offset_start = jax.random.normal(jax.random.fold_in(key, 11), (S, LAT), jnp.float32)
    offset_start = jnp.clip(offset_start, -6.0, 6.0)
    pattern = sign_pattern(key)
    offset_start = offset_start.at[0, :].set(pattern)
    offset_start = offset_start.at[SHARD_KEY_COUNT, :].set(pattern * (1.0 - 2.0 / 360.0))
    return offset_start


def draw_latents(key, part):
    return shared_latents(key).astype(jnp.bfloat16)


def draw_queries(key, part):
    pattern = sign_pattern(key)
    value_rows = jax.random.normal(jax.random.fold_in(key, 13), (QUERY_TOTAL, HEAD_TOTAL, LAT), jnp.float32)
    value_rows = jnp.clip(value_rows, -6.0, 6.0)
    unit = 1.0 / (192.0 ** (-0.5) * 4.0 * LAT)
    for cache_position, target_score in enumerate((120.0, 240.0, 360.0)):
        value_rows = value_rows.at[cache_position, 0, :].set(target_score * unit * pattern)
    return value_rows.astype(jnp.bfloat16)


def draw_query_pos(key, part):
    spacing = jax.random.randint(jax.random.fold_in(key, 17), (QUERY_TOTAL,), 1, 5, jnp.int32)
    after = jnp.cumsum(spacing[::-1])[::-1] - spacing
    return (S - 1 - after).astype(jnp.int32)


def draw_valid_keys(key, part):
    shard_total = S // SHARD_KEY_COUNT
    counts = jax.random.randint(jax.random.fold_in(key, 23), (shard_total,), SHARD_KEY_COUNT // 2, SHARD_KEY_COUNT + 1, jnp.int32)
    order = jax.random.permutation(jax.random.fold_in(key, 29), shard_total)
    counts = counts.at[order[0]].set(SHARD_KEY_COUNT)
    counts = counts.at[order[1]].set(SHARD_KEY_COUNT // 2)
    return counts.astype(jnp.int32)


def block_levels(rng, shape, split, least, top_value):
    gain, own = 1.0, jax.random.fold_in(rng, 6)
    for position, blocks in split:
        steps = jnp.exp(jax.random.uniform(jax.random.fold_in(own, position), (blocks,), jnp.float32, least / len(split), top_value / len(split)))
        gain = gain * jnp.repeat(steps, shape[position] // blocks).reshape([-1 if axis == position else 1 for axis in range(len(shape))])
    return gain


def noise(stream_key, extent, width, most, split=(), kind=jnp.bfloat16):
    loudness = block_levels(stream_key, extent, split, -0.22, 0.18) if split else 1.0
    entries = jax.random.normal(stream_key, extent, jnp.float32) * width * loudness
    return jnp.minimum(jnp.maximum(entries, -most), most).astype(kind)


def setup_inputs(seed: int = 0) -> dict:
    arg_keys = jax.random.split(jax.random.key(seed), 7)
    queries = draw_queries(jax.random.fold_in(arg_keys[6], 71), 0)
    query_pos = draw_query_pos(jax.random.fold_in(arg_keys[6], 71), 0)
    latents = draw_latents(jax.random.fold_in(arg_keys[6], 71), 0)
    valid_keys = draw_valid_keys(jax.random.fold_in(arg_keys[6], 71), 0)
    output_gradient = noise(arg_keys[4], (QUERY_TOTAL, HEAD_TOTAL, LATENT_WIDTH), 100.0, 600.0, ((0, 128), (1, 8)))
    kv_down = noise(arg_keys[5], (D, LAT), D ** -0.5, 0.0625, ((0, 8),))
    return dict(queries=queries, query_pos=query_pos, latents=latents, valid_keys=valid_keys, output_gradient=output_gradient, kv_down=kv_down)


score_scale = 192.0 ** -0.5


def reference(queries, query_pos, latents, valid_keys, output_gradient, kv_down):
    total_keys = latents.shape[0]
    key_pos = jnp.arange(total_keys, dtype=jnp.int32)
    shard_index = key_pos // SHARD_KEY_COUNT
    local_index = key_pos % SHARD_KEY_COUNT
    key_valid = local_index < valid_keys[shard_index]
    visible = key_valid[None, :] & (key_pos[None, :] <= query_pos[:, None])
    keys_wide = latents.astype(jnp.float32)
    value_rows = latents[:, :LATENT_WIDTH].astype(jnp.float32)
    group_count = queries.shape[1] // HEADS_DEV

    def one_group(running, group):
        first_head = (group * HEADS_DEV).astype(jnp.int32)
        block_query = lax.dynamic_slice_in_dim(queries, first_head, HEADS_DEV, 1).astype(jnp.float32)
        block_grad = lax.dynamic_slice_in_dim(output_gradient, first_head, HEADS_DEV, 1).astype(jnp.float32)
        scores = jnp.einsum("qhc,kc->qhk", block_query, keys_wide) * score_scale
        scores = jnp.where(visible[:, None, :], scores, -jnp.inf)
        row_max = jnp.max(scores, axis=-1, keepdims=True)
        lse = row_max + jnp.log(jnp.sum(jnp.exp(scores - row_max), axis=-1, keepdims=True))
        probs = jnp.exp(scores - lse)
        dprobs = jnp.einsum("mcg,dg->mcd", block_grad, value_rows)
        delta_rows = jnp.sum(probs * dprobs, axis=-1, keepdims=True)
        dscores = probs * (dprobs - delta_rows)
        probs_b = lax.optimization_barrier(probs.astype(jnp.bfloat16)).astype(jnp.float32)
        dscores_b = lax.optimization_barrier(dscores.astype(jnp.bfloat16)).astype(jnp.float32)
        key_contribution = jnp.einsum("qhk,qhc->kc", dscores_b, block_query) * score_scale
        value_contribution = jnp.einsum("qhk,qhv->kv", probs_b, block_grad)
        partial_product = jnp.concatenate([key_contribution[:, :LATENT_WIDTH] + value_contribution, key_contribution[:, LATENT_WIDTH:]], axis=1)
        return running + partial_product, None

    latent_grad, _ = lax.scan(one_group, jnp.zeros((total_keys, LAT), jnp.float32), jnp.arange(group_count, dtype=jnp.int32))
    input_grad = lax.dot_general(latent_grad.astype(jnp.bfloat16), kv_down, (((1,), (1,)), ((), ())), preferred_element_type=jnp.float32).astype(jnp.bfloat16)
    return latent_grad, input_grad
```

```python
import jax
import jax.numpy as jnp
from jax import lax
from jax.experimental import pallas as pl
from jax.experimental.pallas import tpu as pltpu
from jax.sharding import Mesh
from jax.sharding import PartitionSpec as P

AXES = ("x", "zh", "zl", "y", "c")
HEAD = ("x", "zh")
SEQ = ("zl", "y", "c")
NX, NZ, NY = 4, 8, 8
HEADS = 16
KEYS = 256
VAL = 512
LAT = 576
BLOCK = 1152
SPAN = NY * HEADS
PART = 288
SPLIT = ((0, 128), (128, 160))
MESH = pl.DeviceIdType.MESH

score_scale = 192.0 ** (-0.5)


def at(**moved):
    return tuple(moved[a] if a in moved else lax.axis_index(a) for a in AXES)


def dot(a, b):
    return jnp.dot(a, b, preferred_element_type=jnp.float32)


def dot_t(a, b):
    return lax.dot_general(a, b, (((1,), (1,)), ((), ())), preferred_element_type=jnp.float32)


def kernel(
    qpos_ref, valid_ref, q_ref, g_ref, lat_ref, out_ref,
    rows, keys, krot, vis, pbuf, dbuf, pb, dsb, stat, stat_z, stat_y, stat_f,
    s1, r1, s2, r2, s3, r3, fin,
    g_recv, g_send, k_recv, k_send, z_recv, z_send, y_recv, y_send, f_recv, f_send,
    r1_recv, r1_send, r2_recv, r2_send, r3_recv, r3_send, r4_recv, r4_send,
):
    x, zh, zl, y, c = (lax.axis_index(a) for a in AXES)
    mine = zl * NY + y
    y_up, y_down = lax.rem(y + 1, NY), lax.rem(y + NY - 1, NY)

    def remote(src, dst, send, recv, to):
        return pltpu.make_async_remote_copy(
            src_ref=src, dst_ref=dst, send_sem=send, recv_sem=recv, device_id=to, device_id_type=MESH
        )

    y_peers = [at(y=lax.rem(y + d, NY)) for d in range(1, NY)]
    z_peers = [lax.rem(zl + d, NZ) for d in range(1, NZ)]
    x_peers = [lax.rem(x + d, NX) for d in range(1, NX)]
    sibling = at(c=1 - c)
    across = at(zh=1 - zh)

    barrier = pltpu.get_barrier_semaphore()
    everyone = (
        y_peers + [at(zl=z) for z in z_peers] + [at(x=k) for k in x_peers] + [sibling, across]
    )
    for peer in everyone:
        pl.semaphore_signal(barrier, inc=1, device_id=peer, device_id_type=MESH)

    rows[mine, :, 0:VAL] = q_ref[0, :, 0:VAL]
    rows[mine, :, VAL : 2 * VAL] = g_ref[0]
    rot = q_ref[0, :, VAL:LAT]
    rows[mine, :, 2 * VAL : BLOCK] = jnp.concatenate([rot, rot], axis=1)
    keys[c, :, 0:VAL] = lat_ref[:, 0:VAL]
    local = lax.broadcasted_iota(jnp.int32, (KEYS, 64), 0)
    flag = jnp.where(local < valid_ref[0], 1.0, 0.0).astype(jnp.bfloat16)
    keys[c, :, VAL:640] = jnp.concatenate([lat_ref[:, VAL:LAT], flag], axis=1)

    pl.semaphore_wait(barrier, len(everyone))

    def send_rows(source, to):
        remote(rows.at[source], rows.at[source], g_send.at[0], g_recv.at[source], to).start()

    def wait_rows(source):
        remote(rows.at[source], rows.at[source], g_send.at[0], g_recv.at[source], sibling).wait_recv()

    send_rows(mine, at(y=y_up))
    send_rows(mine, at(y=y_down))
    for d in range(1, NZ):
        pl.when(zl + d < NZ)(lambda: send_rows(mine, at(zl=zl + d)))
        pl.when(zl - d >= 0)(lambda: send_rows(mine, at(zl=zl - d)))
    swap = remote(keys.at[c], keys.at[c], k_send.at[0], k_recv.at[0], sibling)
    swap.start()
    swap.wait_recv()
    for half in range(2):
        tail = keys[half, :, VAL:640].astype(jnp.float32)
        lane = lax.broadcasted_iota(jnp.int32, (KEYS, 128), 1)
        krot[half * KEYS : (half + 1) * KEYS] = jnp.where(lane < 64, tail, 0.0).astype(jnp.bfloat16)
        vis[half * KEYS : (half + 1) * KEYS] = jnp.broadcast_to(tail[:, 64:65], (KEYS, 128))

    def first_pass(zs):
        chunk = rows.at[pl.ds(zs * NY, NY)]
        values = keys[:, :, 0:VAL].reshape(2 * KEYS, VAL)
        s = dot_t(values, chunk[:, :, 0:VAL].reshape(SPAN, VAL))
        s = s + dot_t(krot[...], chunk[:, :, 2 * VAL : BLOCK].reshape(SPAN, 128))
        lane = lax.broadcasted_iota(jnp.int32, (1, SPAN), 1)
        qpos = jnp.zeros((1, SPAN), jnp.int32)
        for k in range(NY):
            qpos = jnp.where(lane // HEADS == k, qpos_ref[zs * 2 * NY + 2 * k + c], qpos)
        key_pos = lax.broadcasted_iota(jnp.int32, (2 * KEYS, SPAN), 0) + mine * 2 * KEYS
        seen = (vis[...] > 0.5) & (key_pos <= qpos)
        s = jnp.where(seen, s * score_scale, -1e30)
        top = jnp.maximum(jnp.max(s, axis=0, keepdims=True), -1e20)
        p = jnp.exp(s - top)
        dp = dot_t(values, chunk[:, :, VAL : 2 * VAL].reshape(SPAN, VAL))
        pbuf[zs] = p
        dbuf[zs] = dp
        stat[zs, 0:1] = top
        stat[zs, 1:2] = jnp.sum(p, axis=0, keepdims=True)
        stat[zs, 2:3] = jnp.sum(p * dp, axis=0, keepdims=True)
        stat[zs, 3:8] = jnp.zeros((5, SPAN), jnp.float32)

        @pl.when(zs != zl)
        def _():
            remote(
                stat.at[zs], stat_z.at[zl], z_send.at[0], z_recv.at[zl], at(zl=zs)
            ).start()

    def slots(group, work):
        def body(k, _):
            d = 2 * group + k // 2
            zs = jnp.where(k % 2 == 0, zl + d, zl - d)
            ok = (d >= 0) & (zs >= 0) & (zs < NZ) & ((d < NZ) & ((d > 0) | (k % 2 == 0)))
            pl.when(ok)(lambda: work(zs))
            return 0

        lax.fori_loop(0, 4, body, 0)

    def inject(zs):
        @pl.when(zs != zl)
        def _():
            source = zs * NY + y
            wait_rows(source)
            send_rows(source, at(y=y_up))
            send_rows(source, at(y=y_down))

    def pass_on(e):
        def work(zs):
            even = lax.rem(zs, 2) == 0
            rising = zs * NY + lax.rem(y + NY - e, NY)
            falling = zs * NY + lax.rem(y + e, NY)
            if e <= 3:
                wait_rows(rising)
                if e < 3:
                    send_rows(rising, at(y=y_up))
                else:
                    pl.when(even)(lambda: send_rows(rising, at(y=y_up)))
                wait_rows(falling)
                if e < 3:
                    send_rows(falling, at(y=y_down))
                else:
                    pl.when(jnp.logical_not(even))(lambda: send_rows(falling, at(y=y_down)))
            else:
                wait_rows(rising)

        return work

    def step(t, _):
        slots(t, inject)
        for e in range(1, 5):
            pl.when((t - e >= 0) & (t - e <= 3))(lambda e=e: slots(t - e, pass_on(e)))
        pl.when(t >= 4)(lambda: slots(t - 4, first_pass))
        return 0

    lax.fori_loop(0, 8, step, 0)

    def merged(parts):
        top = parts[0][0:1]
        for part in parts[1:]:
            top = jnp.maximum(top, part[0:1])
        total = jnp.zeros_like(top)
        weighted = jnp.zeros_like(top)
        for part in parts:
            gain = jnp.exp(part[0:1] - top)
            total = total + part[1:2] * gain
            weighted = weighted + part[2:3] * gain
        return top, total, weighted

    stat_z[zl] = stat[zl]
    for z in z_peers:
        remote(stat.at[0], stat_z.at[z], z_send.at[0], z_recv.at[z], sibling).wait_recv()
    top, total, weighted = merged([stat_z[k] for k in range(NZ)])
    stat_y[y, 0:1] = top
    stat_y[y, 1:2] = total
    stat_y[y, 2:3] = weighted
    stat_y[y, 3:8] = jnp.zeros((5, SPAN), jnp.float32)
    for d in range(1, NY):
        remote(
            stat_y.at[y], stat_y.at[y], y_send.at[0], y_recv.at[y], at(y=lax.rem(y + d, NY))
        ).start()
    for d in range(1, NY):
        k = lax.rem(y + d, NY)
        remote(stat_y.at[k], stat_y.at[k], y_send.at[0], y_recv.at[k], sibling).wait_recv()
    top, total, weighted = merged([stat_y[k] for k in range(NY)])
    stat_f[zl, 0:1] = top + jnp.log(total)
    stat_f[zl, 1:2] = weighted / total
    stat_f[zl, 2:8] = jnp.zeros((6, SPAN), jnp.float32)
    for z in z_peers:
        remote(stat_f.at[zl], stat_f.at[zl], f_send.at[0], f_recv.at[zl], at(zl=z)).start()

    def second_pass(zs):
        gain = jnp.exp(stat[zs, 0:1] - stat_f[zs, 0:1])
        p = pbuf[zs] * gain
        pb[zs] = p.astype(jnp.bfloat16)
        dsb[zs] = (p * (dbuf[zs] - stat_f[zs, 1:2])).astype(jnp.bfloat16)

    def each(k, _):
        zs = lax.rem(zl + k, NZ)

        @pl.when(k > 0)
        def _():
            remote(stat_f.at[zs], stat_f.at[zs], f_send.at[0], f_recv.at[zs], sibling).wait_recv()

        second_pass(zs)
        return 0

    lax.fori_loop(0, NZ, each, 0)

    def gradient(half, piece):
        first = pl.multiple_of(half * KEYS, KEYS)
        lo = piece * 256
        value = jnp.zeros((KEYS, 256), jnp.float32)
        key = jnp.zeros((KEYS, 256), jnp.float32)
        turn = jnp.zeros((KEYS, 128), jnp.float32)
        for k in range(NZ):
            chunk = rows.at[k * NY : (k + 1) * NY]
            ds_k = dsb[k, pl.ds(first, KEYS)]
            key = key + dot(ds_k, chunk[:, :, lo : lo + 256].reshape(SPAN, 256))
            value = value + dot(
                pb[k, pl.ds(first, KEYS)],
                chunk[:, :, VAL + lo : VAL + lo + 256].reshape(SPAN, 256),
            )
            if piece == 1:
                turn = turn + dot(ds_k, chunk[:, :, 2 * VAL : BLOCK].reshape(SPAN, 128))
        both = (key * score_scale + value).reshape(NX, 64, 256)
        tiles = [both[:, :, 0:128], both[:, :, 128:256]]
        if piece == 1:
            turn = (turn * score_scale).reshape(NX, 2, 32, 128)
            lane = lax.broadcasted_iota(jnp.int32, (NX, 32, 128), 2)
            tiles.append(jnp.where(lane < 64, turn[:, 0], turn[:, 1]))
        return jnp.concatenate(tiles, axis=1)

    for piece, (lo, size) in enumerate(SPLIT):
        s1[:, lo : lo + size] = gradient(1 - c, piece).astype(jnp.bfloat16)
        part = pl.ds(lo, size)
        remote(
            s1.at[:, part], r1.at[:, part], r1_send.at[piece], r1_recv.at[piece], sibling
        ).start()
    for piece, (lo, size) in enumerate(SPLIT):
        own = gradient(c, piece)
        part = pl.ds(lo, size)
        remote(
            s1.at[:, part], r1.at[:, part], r1_send.at[piece], r1_recv.at[piece], sibling
        ).wait()
        s2[:, lo : lo + size] = (own + r1[:, lo : lo + size].astype(jnp.float32)).astype(
            jnp.bfloat16
        )
        for k in x_peers:
            remote(
                s2.at[k, part], r2.at[x, part], r2_send.at[piece], r2_recv.at[piece, x], at(x=k)
            ).start()
    for piece, (lo, size) in enumerate(SPLIT):
        part = pl.ds(lo, size)
        for k in x_peers:
            remote(
                s2.at[k, part], r2.at[k, part], r2_send.at[piece], r2_recv.at[piece, k], at(x=k)
            ).wait_recv()
        total = s2[x, lo : lo + size].astype(jnp.float32)
        for k in x_peers:
            total = total + r2[k, lo : lo + size].astype(jnp.float32)
        s3[lo : lo + size] = total.astype(jnp.bfloat16)
        remote(s3.at[part], r3.at[part], r3_send.at[piece], r3_recv.at[piece], across).start()
    for piece, (lo, size) in enumerate(SPLIT):
        part = pl.ds(lo, size)
        remote(s3.at[part], r3.at[part], r3_send.at[piece], r3_recv.at[piece], across).wait()
        total = s3[lo : lo + size].astype(jnp.float32) + r3[lo : lo + size].astype(jnp.float32)
        fin[x, lo : lo + size] = total.astype(jnp.bfloat16)
        for k in x_peers:
            remote(
                fin.at[x, part], fin.at[x, part], r4_send.at[piece], r4_recv.at[piece, x], at(x=k)
            ).start()
    for piece, (lo, size) in enumerate(SPLIT):
        part = pl.ds(lo, size)
        for k in x_peers:
            remote(
                fin.at[k, part], fin.at[k, part], r4_send.at[piece], r4_recv.at[piece, k], at(x=k)
            ).wait_recv()
    for k in range(NX):
        for tile in range(4):
            out_ref[k * 64 : (k + 1) * 64, tile * 128 : (tile + 1) * 128] = fin[
                k, tile * 64 : (tile + 1) * 64
            ]
        out_ref[k * 64 : k * 64 + 32, VAL:LAT] = fin[k, 256:288, 0:64]
        out_ref[k * 64 + 32 : (k + 1) * 64, VAL:LAT] = fin[k, 256:288, 64:128]

    most = rows.at[pl.ds(0, NZ * NY - 1)]
    remote(most, most, g_send.at[0], g_recv.at[0], sibling).wait_send()
    swap.wait_send()
    for buffer, sem in ((stat, z_send), (stat_y, y_send), (stat_f, f_send)):
        seven = buffer.at[pl.ds(0, 7)]
        remote(seven, seven, sem.at[0], z_recv.at[0], sibling).wait_send()
    for piece, (lo, size) in enumerate(SPLIT):
        three = s2.at[pl.ds(0, 3), pl.ds(lo, size)]
        remote(three, three, r2_send.at[piece], r2_recv.at[piece, 0], sibling).wait_send()
        remote(three, three, r4_send.at[piece], r4_recv.at[piece, 0], sibling).wait_send()


def latent_gradient(query_pos, valid_keys, queries, output_gradient, latents):
    bf16, f32 = jnp.bfloat16, jnp.float32
    vmem, smem = pl.BlockSpec(memory_space=pltpu.VMEM), pl.BlockSpec(memory_space=pltpu.SMEM)
    dma = pltpu.SemaphoreType.DMA
    return pl.pallas_call(
        kernel,
        out_shape=jax.ShapeDtypeStruct((KEYS, LAT), bf16),
        in_specs=[smem, smem, vmem, vmem, vmem],
        out_specs=vmem,
        scratch_shapes=[
            pltpu.VMEM((NZ * NY, HEADS, BLOCK), bf16),
            pltpu.VMEM((2, KEYS, 640), bf16),
            pltpu.VMEM((2 * KEYS, 128), bf16),
            pltpu.VMEM((2 * KEYS, 128), f32),
            pltpu.VMEM((NZ, 2 * KEYS, SPAN), f32),
            pltpu.VMEM((NZ, 2 * KEYS, SPAN), f32),
            pltpu.VMEM((NZ, 2 * KEYS, SPAN), bf16),
            pltpu.VMEM((NZ, 2 * KEYS, SPAN), bf16),
            pltpu.VMEM((NZ, 8, SPAN), f32),
            pltpu.VMEM((NZ, 8, SPAN), f32),
            pltpu.VMEM((NY, 8, SPAN), f32),
            pltpu.VMEM((NZ, 8, SPAN), f32),
            pltpu.VMEM((NX, PART, 128), bf16),
            pltpu.VMEM((NX, PART, 128), bf16),
            pltpu.VMEM((NX, PART, 128), bf16),
            pltpu.VMEM((NX, PART, 128), bf16),
            pltpu.VMEM((PART, 128), bf16),
            pltpu.VMEM((PART, 128), bf16),
            pltpu.VMEM((NX, PART, 128), bf16),
            dma((NZ * NY,)), dma((1,)), dma((1,)), dma((1,)),
            dma((NZ,)), dma((1,)), dma((NY,)), dma((1,)), dma((NZ,)), dma((1,)),
            dma((2,)), dma((2,)), dma((2, NX)), dma((2,)),
            dma((2,)), dma((2,)), dma((2, NX)), dma((2,)),
        ],
        compiler_params=pltpu.CompilerParams(
            collective_id=0, has_side_effects=True, vmem_limit_bytes=40 * 2**20
        ),
        cost_estimate=pl.CostEstimate(
            flops=2_500_000_000, bytes_accessed=1_000_000, transcendentals=600_000
        ),
    )(query_pos, valid_keys, queries, output_gradient, latents)


def shards(queries, query_pos, latents, valid_keys, output_gradient, kv_down):
    latent_b = latent_gradient(query_pos, valid_keys, queries, output_gradient, latents)
    input_grad = lax.dot_general(
        latent_b, kv_down, (((1,), (1,)), ((), ())), preferred_element_type=jnp.float32
    ).astype(jnp.bfloat16)
    return (latent_b.astype(jnp.float32), input_grad)


def solution(mesh):
    torus = Mesh(mesh.devices.reshape(NX, 2, NZ, NY, 2), AXES)
    placed = (
        P(SEQ, HEAD, None),
        P(),
        P(SEQ, None),
        P(SEQ),
        P(SEQ, HEAD, None),
        P(HEAD, None),
    )
    return jax.shard_map(
        shards,
        mesh=torus,
        in_specs=placed,
        out_specs=(P(SEQ, None), P(SEQ, HEAD)),
        check_vma=False,
    )
```

```python
import jax
import jax.numpy as jnp
from jax import lax
from jax.experimental import pallas as pl
from jax.experimental.pallas import tpu as pltpu
from jax.sharding import Mesh
from jax.sharding import PartitionSpec as P

AXES = ("x", "zh", "zl", "y", "c")
HEAD = ("x", "zh")
SEQ = ("zl", "y", "c")
NX, NZ, NY = 4, 8, 8
HEADS = 16
KEYS = 256
VAL = 512
LAT = 576
BLOCK = 1152
GRAD = 640
CUT = 1024
SPAN = NY * HEADS
PART = 288
SPLIT = ((0, 128), (128, 160))
MESH = pl.DeviceIdType.MESH

ORDER = (
    "y01", "z1", "y02", "p0", "z2", "y11", "z3", "y21", "r1", "y12", "z4", "y03",
    "y31", "z5", "r2", "y22", "y13", "z6", "y41", "z7", "r3", "y04", "y32", "y51",
    "c0", "y61", "y23", "r4", "y14", "y42", "y71", "c1", "y52", "y33", "y62", "r5",
    "y24", "y43", "y72", "c2", "y53", "y34", "y63", "r6", "c3", "y73", "y44", "c4",
    "y54", "c5", "y64", "c6", "y74", "r7", "c7",
)

score_scale = 192.0 ** (-0.5)


def at(**moved):
    return tuple(moved[a] if a in moved else lax.axis_index(a) for a in AXES)


def dot(a, b):
    return jnp.dot(a, b, preferred_element_type=jnp.float32)


def dot_t(a, b):
    return lax.dot_general(a, b, (((1,), (1,)), ((), ())), preferred_element_type=jnp.float32)


def kernel(
    qpos_ref, valid_ref, q_ref, g_ref, lat_ref, out_ref,
    rows, keys, krot, vis, pbuf, dbuf, pb, dsb, stat, stat_z, stat_y, stat_f,
    s1, r1, s2, r2, s3, r3, fin,
    g_recv, g_send, h_recv, h_send, t_recv, t_send, k_recv, k_send, z_recv, z_send, y_recv, y_send, f_recv, f_send,
    r1_recv, r1_send, r2_recv, r2_send, r3_recv, r3_send, r4_recv, r4_send,
):
    x, zh, zl, y, c = (lax.axis_index(a) for a in AXES)
    mine = zl * NY + y
    y_up, y_down = lax.rem(y + 1, NY), lax.rem(y + NY - 1, NY)

    def remote(src, dst, send, recv, to):
        return pltpu.make_async_remote_copy(
            src_ref=src, dst_ref=dst, send_sem=send, recv_sem=recv, device_id=to, device_id_type=MESH
        )

    y_peers = [at(y=lax.rem(y + d, NY)) for d in range(1, NY)]
    z_peers = [lax.rem(zl + d, NZ) for d in range(1, NZ)]
    x_peers = [lax.rem(x + d, NX) for d in range(1, NX)]
    sibling = at(c=1 - c)
    across = at(zh=1 - zh)

    barrier = pltpu.get_barrier_semaphore()
    everyone = (
        y_peers + [at(zl=z) for z in z_peers] + [at(x=k) for k in x_peers] + [sibling, across]
    )
    for peer in everyone:
        pl.semaphore_signal(barrier, inc=1, device_id=peer, device_id_type=MESH)

    rows[mine, :, 0:VAL] = q_ref[0, :, 0:VAL]
    rot = q_ref[0, :, VAL:LAT]
    rows[mine, :, VAL:GRAD] = jnp.concatenate([rot, rot], axis=1)
    rows[mine, :, GRAD:BLOCK] = g_ref[0]
    keys[c, :, 0:VAL] = lat_ref[:, 0:VAL]
    local = lax.broadcasted_iota(jnp.int32, (KEYS, 64), 0)
    flag = jnp.where(local < valid_ref[0], 1.0, 0.0).astype(jnp.bfloat16)
    keys[c, :, VAL:640] = jnp.concatenate([lat_ref[:, VAL:LAT], flag], axis=1)

    pl.semaphore_wait(barrier, len(everyone))

    def send_rows(source, to):
        block = rows.at[source, :, pl.ds(0, CUT)]
        remote(block, block, g_send.at[0], g_recv.at[source], to).start()

    def wait_rows(source):
        block = rows.at[source, :, pl.ds(0, CUT)]
        remote(block, block, g_send.at[0], g_recv.at[source], sibling).wait_recv()

    def rest_along_y(k):
        block = rows.at[zl * NY + k, :, pl.ds(CUT, BLOCK - CUT)]
        return block, h_send.at[0], h_recv.at[k]

    def rest_along_z(zs, half):
        block = rows.at[pl.ds(zs * NY + half * 4, 4), :, pl.ds(CUT, BLOCK - CUT)]
        return block, t_recv.at[zs, half]

    def rest_copies(zs, half):
        block, recv = rest_along_z(zs, half)
        up = remote(block, block, t_send.at[zs, half, 0], recv, at(zl=zl + 1))
        down = remote(block, block, t_send.at[zs, half, 1], recv, at(zl=zl - 1))
        return ((zs <= zl) & (zl + 1 < NZ), up), ((zs >= zl) & (zl - 1 >= 0), down)

    def rest_send(zs, half):
        for ok, copy in rest_copies(zs, half):
            pl.when(ok)(copy.start)

    def rest_relay(zs):
        for half in range(2):
            block, recv = rest_along_z(zs, half)
            remote(block, block, t_send.at[0, 0, 0], recv, sibling).wait_recv()
            rest_send(zs, half)

    def rest_drain(zs):
        for half in range(2):
            for ok, copy in rest_copies(zs, half):
                pl.when(ok)(copy.wait_send)

    send_rows(mine, at(y=y_up))
    send_rows(mine, at(y=y_down))
    for d in range(1, NZ):
        pl.when(zl + d < NZ)(lambda: send_rows(mine, at(zl=zl + d)))
        pl.when(zl - d >= 0)(lambda: send_rows(mine, at(zl=zl - d)))
    block, send, recv = rest_along_y(y)
    for peer in y_peers:
        remote(block, block, send, recv, peer).start()
    swap = remote(keys.at[c], keys.at[c], k_send.at[0], k_recv.at[0], sibling)
    swap.start()
    swap.wait_recv()
    for half in range(2):
        tail = keys[half, :, VAL:640].astype(jnp.float32)
        lane = lax.broadcasted_iota(jnp.int32, (KEYS, 128), 1)
        krot[half * KEYS : (half + 1) * KEYS] = jnp.where(lane < 64, tail, 0.0).astype(jnp.bfloat16)
        vis[half * KEYS : (half + 1) * KEYS] = jnp.broadcast_to(tail[:, 64:65], (KEYS, 128))

    def first_pass(zs):
        chunk = rows.at[pl.ds(zs * NY, NY)]
        values = keys[:, :, 0:VAL].reshape(2 * KEYS, VAL)
        s = dot_t(values, chunk[:, :, 0:VAL].reshape(SPAN, VAL))
        s = s + dot_t(krot[...], chunk[:, :, VAL:GRAD].reshape(SPAN, 128))
        lane = lax.broadcasted_iota(jnp.int32, (1, SPAN), 1)
        qpos = jnp.zeros((1, SPAN), jnp.int32)
        for k in range(NY):
            qpos = jnp.where(lane // HEADS == k, qpos_ref[zs * 2 * NY + 2 * k + c], qpos)
        key_pos = lax.broadcasted_iota(jnp.int32, (2 * KEYS, SPAN), 0) + mine * 2 * KEYS
        seen = (vis[...] > 0.5) & (key_pos <= qpos)
        s = jnp.where(seen, s * score_scale, -1e30)
        top = jnp.maximum(jnp.max(s, axis=0, keepdims=True), -1e20)
        p = jnp.exp(s - top)
        dp = dot_t(values, chunk[:, :, GRAD:BLOCK].reshape(SPAN, VAL))
        pbuf[zs] = p
        dbuf[zs] = dp
        stat[zs, 0:1] = top
        stat[zs, 1:2] = jnp.sum(p, axis=0, keepdims=True)
        stat[zs, 2:3] = jnp.sum(p * dp, axis=0, keepdims=True)
        stat[zs, 3:8] = jnp.zeros((5, SPAN), jnp.float32)

        @pl.when(zs != zl)
        def _():
            remote(
                stat.at[zs], stat_z.at[zl], z_send.at[0], z_recv.at[zl], at(zl=zs)
            ).start()

    def places(d, work):
        def body(k, _):
            zs = jnp.where(k == 0, zl + d, zl - d)
            pl.when((zs >= 0) & (zs < NZ))(lambda: work(zs))
            return 0

        if d == 0:
            work(zl)
        else:
            lax.fori_loop(0, 2, body, 0)

    def inject(zs):
        source = zs * NY + y
        wait_rows(source)
        send_rows(source, at(y=y_up))
        send_rows(source, at(y=y_down))

    def pass_on(e):
        def work(zs):
            even = lax.rem(zs, 2) == 0
            rising = zs * NY + lax.rem(y + NY - e, NY)
            falling = zs * NY + lax.rem(y + e, NY)
            if e <= 3:
                wait_rows(rising)
                if e < 3:
                    send_rows(rising, at(y=y_up))
                else:
                    pl.when(even)(lambda: send_rows(rising, at(y=y_up)))
                wait_rows(falling)
                if e < 3:
                    send_rows(falling, at(y=y_down))
                else:
                    pl.when(jnp.logical_not(even))(lambda: send_rows(falling, at(y=y_down)))
            else:
                wait_rows(rising)

        return work

    for event in ORDER:
        kind, d = event[0], int(event[1])
        if kind == "z":
            places(d, inject)
        elif kind == "y":
            places(d, pass_on(int(event[2])))
        elif kind == "r":
            places(d, rest_relay)
        elif kind == "c":
            places(d, first_pass)
        else:
            for k in range(1, NY):
                block, send, recv = rest_along_y(lax.rem(y + k, NY))
                remote(block, block, send, recv, sibling).wait_recv()
            for half in range(2):
                rest_send(zl, half)

    def merged(parts):
        top = parts[0][0:1]
        for part in parts[1:]:
            top = jnp.maximum(top, part[0:1])
        total = jnp.zeros_like(top)
        weighted = jnp.zeros_like(top)
        for part in parts:
            gain = jnp.exp(part[0:1] - top)
            total = total + part[1:2] * gain
            weighted = weighted + part[2:3] * gain
        return top, total, weighted

    stat_z[zl] = stat[zl]
    for z in z_peers:
        remote(stat.at[0], stat_z.at[z], z_send.at[0], z_recv.at[z], sibling).wait_recv()
    top, total, weighted = merged([stat_z[k] for k in range(NZ)])
    stat_y[y, 0:1] = top
    stat_y[y, 1:2] = total
    stat_y[y, 2:3] = weighted
    stat_y[y, 3:8] = jnp.zeros((5, SPAN), jnp.float32)
    for d in range(1, NY):
        remote(
            stat_y.at[y], stat_y.at[y], y_send.at[0], y_recv.at[y], at(y=lax.rem(y + d, NY))
        ).start()
    for d in range(1, NY):
        k = lax.rem(y + d, NY)
        remote(stat_y.at[k], stat_y.at[k], y_send.at[0], y_recv.at[k], sibling).wait_recv()
    top, total, weighted = merged([stat_y[k] for k in range(NY)])
    stat_f[zl, 0:1] = top + jnp.log(total)
    stat_f[zl, 1:2] = weighted / total
    stat_f[zl, 2:8] = jnp.zeros((6, SPAN), jnp.float32)
    for z in z_peers:
        remote(stat_f.at[zl], stat_f.at[zl], f_send.at[0], f_recv.at[zl], at(zl=z)).start()

    def second_pass(zs):
        gain = jnp.exp(stat[zs, 0:1] - stat_f[zs, 0:1])
        p = pbuf[zs] * gain
        pb[zs] = p.astype(jnp.bfloat16)
        dsb[zs] = (p * (dbuf[zs] - stat_f[zs, 1:2])).astype(jnp.bfloat16)

    def each(k, _):
        zs = lax.rem(zl + k, NZ)

        @pl.when(k > 0)
        def _():
            remote(stat_f.at[zs], stat_f.at[zs], f_send.at[0], f_recv.at[zs], sibling).wait_recv()

        second_pass(zs)
        return 0

    lax.fori_loop(0, NZ, each, 0)

    def gradient(half, piece):
        first = pl.multiple_of(half * KEYS, KEYS)
        lo = piece * 256
        value = jnp.zeros((KEYS, 256), jnp.float32)
        key = jnp.zeros((KEYS, 256), jnp.float32)
        turn = jnp.zeros((KEYS, 128), jnp.float32)
        for k in range(NZ):
            chunk = rows.at[k * NY : (k + 1) * NY]
            ds_k = dsb[k, pl.ds(first, KEYS)]
            key = key + dot(ds_k, chunk[:, :, lo : lo + 256].reshape(SPAN, 256))
            value = value + dot(
                pb[k, pl.ds(first, KEYS)],
                chunk[:, :, GRAD + lo : GRAD + lo + 256].reshape(SPAN, 256),
            )
            if piece == 1:
                turn = turn + dot(ds_k, chunk[:, :, VAL:GRAD].reshape(SPAN, 128))
        both = (key * score_scale + value).reshape(NX, 64, 256)
        tiles = [both[:, :, 0:128], both[:, :, 128:256]]
        if piece == 1:
            turn = (turn * score_scale).reshape(NX, 2, 32, 128)
            lane = lax.broadcasted_iota(jnp.int32, (NX, 32, 128), 2)
            tiles.append(jnp.where(lane < 64, turn[:, 0], turn[:, 1]))
        return jnp.concatenate(tiles, axis=1)

    for piece, (lo, size) in enumerate(SPLIT):
        s1[:, lo : lo + size] = gradient(1 - c, piece).astype(jnp.bfloat16)
        part = pl.ds(lo, size)
        remote(
            s1.at[:, part], r1.at[:, part], r1_send.at[piece], r1_recv.at[piece], sibling
        ).start()
    for piece, (lo, size) in enumerate(SPLIT):
        own = gradient(c, piece)
        part = pl.ds(lo, size)
        remote(
            s1.at[:, part], r1.at[:, part], r1_send.at[piece], r1_recv.at[piece], sibling
        ).wait()
        s2[:, lo : lo + size] = (own + r1[:, lo : lo + size].astype(jnp.float32)).astype(
            jnp.bfloat16
        )
        for k in x_peers:
            remote(
                s2.at[k, part], r2.at[x, part], r2_send.at[piece], r2_recv.at[piece, x], at(x=k)
            ).start()
    for piece, (lo, size) in enumerate(SPLIT):
        part = pl.ds(lo, size)
        for k in x_peers:
            remote(
                s2.at[k, part], r2.at[k, part], r2_send.at[piece], r2_recv.at[piece, k], at(x=k)
            ).wait_recv()
        total = s2[x, lo : lo + size].astype(jnp.float32)
        for k in x_peers:
            total = total + r2[k, lo : lo + size].astype(jnp.float32)
        s3[lo : lo + size] = total.astype(jnp.bfloat16)
        remote(s3.at[part], r3.at[part], r3_send.at[piece], r3_recv.at[piece], across).start()
    for piece, (lo, size) in enumerate(SPLIT):
        part = pl.ds(lo, size)
        remote(s3.at[part], r3.at[part], r3_send.at[piece], r3_recv.at[piece], across).wait()
        total = s3[lo : lo + size].astype(jnp.float32) + r3[lo : lo + size].astype(jnp.float32)
        fin[x, lo : lo + size] = total.astype(jnp.bfloat16)
        for k in x_peers:
            remote(
                fin.at[x, part], fin.at[x, part], r4_send.at[piece], r4_recv.at[piece, x], at(x=k)
            ).start()
    for piece, (lo, size) in enumerate(SPLIT):
        part = pl.ds(lo, size)
        for k in x_peers:
            remote(
                fin.at[k, part], fin.at[k, part], r4_send.at[piece], r4_recv.at[piece, k], at(x=k)
            ).wait_recv()
    for k in range(NX):
        for tile in range(4):
            out_ref[k * 64 : (k + 1) * 64, tile * 128 : (tile + 1) * 128] = fin[
                k, tile * 64 : (tile + 1) * 64
            ]
        out_ref[k * 64 : k * 64 + 32, VAL:LAT] = fin[k, 256:288, 0:64]
        out_ref[k * 64 + 32 : (k + 1) * 64, VAL:LAT] = fin[k, 256:288, 64:128]

    for zs in range(NZ):
        rest_drain(zs)
    block, send, recv = rest_along_y(y)
    seven = rows.at[pl.ds(0, 7), :, pl.ds(CUT, BLOCK - CUT)]
    remote(seven, seven, send, recv, sibling).wait_send()
    most = rows.at[pl.ds(0, NZ * NY - 1), :, pl.ds(0, CUT)]
    remote(most, most, g_send.at[0], g_recv.at[0], sibling).wait_send()
    swap.wait_send()
    for buffer, sem in ((stat, z_send), (stat_y, y_send), (stat_f, f_send)):
        seven = buffer.at[pl.ds(0, 7)]
        remote(seven, seven, sem.at[0], z_recv.at[0], sibling).wait_send()
    for piece, (lo, size) in enumerate(SPLIT):
        three = s2.at[pl.ds(0, 3), pl.ds(lo, size)]
        remote(three, three, r2_send.at[piece], r2_recv.at[piece, 0], sibling).wait_send()
        remote(three, three, r4_send.at[piece], r4_recv.at[piece, 0], sibling).wait_send()


def latent_gradient(query_pos, valid_keys, queries, output_gradient, latents):
    bf16, f32 = jnp.bfloat16, jnp.float32
    vmem, smem = pl.BlockSpec(memory_space=pltpu.VMEM), pl.BlockSpec(memory_space=pltpu.SMEM)
    dma = pltpu.SemaphoreType.DMA
    return pl.pallas_call(
        kernel,
        out_shape=jax.ShapeDtypeStruct((KEYS, LAT), bf16),
        in_specs=[smem, smem, vmem, vmem, vmem],
        out_specs=vmem,
        scratch_shapes=[
            pltpu.VMEM((NZ * NY, HEADS, BLOCK), bf16),
            pltpu.VMEM((2, KEYS, 640), bf16),
            pltpu.VMEM((2 * KEYS, 128), bf16),
            pltpu.VMEM((2 * KEYS, 128), f32),
            pltpu.VMEM((NZ, 2 * KEYS, SPAN), f32),
            pltpu.VMEM((NZ, 2 * KEYS, SPAN), f32),
            pltpu.VMEM((NZ, 2 * KEYS, SPAN), bf16),
            pltpu.VMEM((NZ, 2 * KEYS, SPAN), bf16),
            pltpu.VMEM((NZ, 8, SPAN), f32),
            pltpu.VMEM((NZ, 8, SPAN), f32),
            pltpu.VMEM((NY, 8, SPAN), f32),
            pltpu.VMEM((NZ, 8, SPAN), f32),
            pltpu.VMEM((NX, PART, 128), bf16),
            pltpu.VMEM((NX, PART, 128), bf16),
            pltpu.VMEM((NX, PART, 128), bf16),
            pltpu.VMEM((NX, PART, 128), bf16),
            pltpu.VMEM((PART, 128), bf16),
            pltpu.VMEM((PART, 128), bf16),
            pltpu.VMEM((NX, PART, 128), bf16),
            dma((NZ * NY,)), dma((1,)), dma((NY,)), dma((1,)), dma((NZ, 2)), dma((NZ, 2, 2)),
            dma((1,)), dma((1,)),
            dma((NZ,)), dma((1,)), dma((NY,)), dma((1,)), dma((NZ,)), dma((1,)),
            dma((2,)), dma((2,)), dma((2, NX)), dma((2,)),
            dma((2,)), dma((2,)), dma((2, NX)), dma((2,)),
        ],
        compiler_params=pltpu.CompilerParams(
            collective_id=0, has_side_effects=True, vmem_limit_bytes=40 * 2**20
        ),
        cost_estimate=pl.CostEstimate(
            flops=2_500_000_000, bytes_accessed=1_000_000, transcendentals=600_000
        ),
    )(query_pos, valid_keys, queries, output_gradient, latents)


def shards(queries, query_pos, latents, valid_keys, output_gradient, kv_down):
    latent_b = latent_gradient(query_pos, valid_keys, queries, output_gradient, latents)
    input_grad = lax.dot_general(
        latent_b, kv_down, (((1,), (1,)), ((), ())), preferred_element_type=jnp.float32
    ).astype(jnp.bfloat16)
    return (latent_b.astype(jnp.float32), input_grad)


def solution(mesh):
    torus = Mesh(mesh.devices.reshape(NX, 2, NZ, NY, 2), AXES)
    placed = (
        P(SEQ, HEAD, None),
        P(),
        P(SEQ, None),
        P(SEQ),
        P(SEQ, HEAD, None),
        P(HEAD, None),
    )
    return jax.shard_map(
        shards,
        mesh=torus,
        in_specs=placed,
        out_specs=(P(SEQ, None), P(SEQ, HEAD)),
        check_vma=False,
    )
```

```python
import jax
import jax.numpy as jnp
from jax import lax
from jax.experimental import pallas as pl
from jax.experimental.pallas import tpu as pltpu
from jax.sharding import Mesh
from jax.sharding import PartitionSpec as P

AXES = ("x", "zh", "zl", "y", "c")
HEAD = ("x", "zh")
SEQ = ("zl", "y", "c")
NX, NZ, NY = 4, 8, 8
HEADS = 16
KEYS = 256
VAL = 512
LAT = 576
BLOCK = 1152
GRAD = 640
CUT = 1024
SPAN = NY * HEADS
PART = 288
SPLIT = ((0, 128), (128, 160))
MESH = pl.DeviceIdType.MESH

ORDER = (
    "y01", "z1", "p0", "y02", "z2", "y11", "z3", "y03", "r1", "z4", "y21", "z5",
    "y12", "y31", "r2", "z6", "y41", "z7", "y51", "y22", "r3", "y32", "y61", "y42",
    "y71", "y13", "y52", "r4", "y23", "y33", "y04", "y62", "y72", "y43", "c0", "r5",
    "y14", "y53", "c1", "y63", "y24", "y34", "c3", "y73", "r6", "c2", "y44", "y54",
    "c4", "c5", "y64", "c6", "y74", "r7", "c7",
)

score_scale = 192.0 ** (-0.5)


def at(**moved):
    return tuple(moved[a] if a in moved else lax.axis_index(a) for a in AXES)


def dot(a, b):
    return jnp.dot(a, b, preferred_element_type=jnp.float32)


def dot_t(a, b):
    return lax.dot_general(a, b, (((1,), (1,)), ((), ())), preferred_element_type=jnp.float32)


def kernel(
    qpos_ref, valid_ref, q_ref, g_ref, lat_ref, out_ref,
    rows, keys, krot, vis, pbuf, dbuf, pb, dsb, stat, stat_z, stat_y, stat_f,
    s1, r1, s2, r2, s3, r3, fin,
    g_recv, g_send, h_recv, h_send, t_recv, t_send, k_recv, k_send, z_recv, z_send, y_recv, y_send, f_recv, f_send,
    r1_recv, r1_send, r2_recv, r2_send, r3_recv, r3_send, r4_recv, r4_send,
):
    x, zh, zl, y, c = (lax.axis_index(a) for a in AXES)
    mine = zl * NY + y
    y_up, y_down = lax.rem(y + 1, NY), lax.rem(y + NY - 1, NY)

    def remote(src, dst, send, recv, to):
        return pltpu.make_async_remote_copy(
            src_ref=src, dst_ref=dst, send_sem=send, recv_sem=recv, device_id=to, device_id_type=MESH
        )

    y_peers = [at(y=lax.rem(y + d, NY)) for d in range(1, NY)]
    z_peers = [lax.rem(zl + d, NZ) for d in range(1, NZ)]
    x_peers = [lax.rem(x + d, NX) for d in range(1, NX)]
    sibling = at(c=1 - c)
    across = at(zh=1 - zh)

    barrier = pltpu.get_barrier_semaphore()
    everyone = (
        y_peers + [at(zl=z) for z in z_peers] + [at(x=k) for k in x_peers] + [sibling, across]
    )
    for peer in everyone:
        pl.semaphore_signal(barrier, inc=1, device_id=peer, device_id_type=MESH)

    rows[mine, :, 0:VAL] = q_ref[0, :, 0:VAL]
    rot = q_ref[0, :, VAL:LAT]
    rows[mine, :, VAL:GRAD] = jnp.concatenate([rot, rot], axis=1)
    rows[mine, :, GRAD:BLOCK] = g_ref[0]
    keys[c, :, 0:VAL] = lat_ref[:, 0:VAL]
    local = lax.broadcasted_iota(jnp.int32, (KEYS, 64), 0)
    flag = jnp.where(local < valid_ref[0], 1.0, 0.0).astype(jnp.bfloat16)
    keys[c, :, VAL:640] = jnp.concatenate([lat_ref[:, VAL:LAT], flag], axis=1)

    pl.semaphore_wait(barrier, len(everyone))

    def send_rows(source, to):
        block = rows.at[source, :, pl.ds(0, CUT)]
        remote(block, block, g_send.at[0], g_recv.at[source], to).start()

    def wait_rows(source):
        block = rows.at[source, :, pl.ds(0, CUT)]
        remote(block, block, g_send.at[0], g_recv.at[source], sibling).wait_recv()

    def rest_along_y(k):
        block = rows.at[zl * NY + k, :, pl.ds(CUT, BLOCK - CUT)]
        return block, h_send.at[0], h_recv.at[k]

    def rest_along_z(zs, half):
        block = rows.at[pl.ds(zs * NY + half * 4, 4), :, pl.ds(CUT, BLOCK - CUT)]
        return block, t_recv.at[zs, half]

    def rest_copies(zs, half):
        block, recv = rest_along_z(zs, half)
        up = remote(block, block, t_send.at[zs, half, 0], recv, at(zl=zl + 1))
        down = remote(block, block, t_send.at[zs, half, 1], recv, at(zl=zl - 1))
        return ((zs <= zl) & (zl + 1 < NZ), up), ((zs >= zl) & (zl - 1 >= 0), down)

    def rest_send(zs, half):
        for ok, copy in rest_copies(zs, half):
            pl.when(ok)(copy.start)

    def rest_relay(zs):
        for half in range(2):
            block, recv = rest_along_z(zs, half)
            remote(block, block, t_send.at[0, 0, 0], recv, sibling).wait_recv()
            rest_send(zs, half)

    def rest_drain(zs):
        for half in range(2):
            for ok, copy in rest_copies(zs, half):
                pl.when(ok)(copy.wait_send)

    send_rows(mine, at(y=y_up))
    send_rows(mine, at(y=y_down))
    for d in range(1, NZ):
        pl.when(zl + d < NZ)(lambda: send_rows(mine, at(zl=zl + d)))
        pl.when(zl - d >= 0)(lambda: send_rows(mine, at(zl=zl - d)))
    block, send, recv = rest_along_y(y)
    for peer in y_peers:
        remote(block, block, send, recv, peer).start()
    swap = remote(keys.at[c], keys.at[c], k_send.at[0], k_recv.at[0], sibling)
    swap.start()

    def take_keys():
        swap.wait_recv()
        for half in range(2):
            tail = keys[half, :, VAL:640].astype(jnp.float32)
            lane = lax.broadcasted_iota(jnp.int32, (KEYS, 128), 1)
            krot[half * KEYS : (half + 1) * KEYS] = jnp.where(lane < 64, tail, 0.0).astype(jnp.bfloat16)
            vis[half * KEYS : (half + 1) * KEYS] = jnp.broadcast_to(tail[:, 64:65], (KEYS, 128))

    def first_pass(zs):
        chunk = rows.at[pl.ds(zs * NY, NY)]
        values = keys[:, :, 0:VAL].reshape(2 * KEYS, VAL)
        s = dot_t(values, chunk[:, :, 0:VAL].reshape(SPAN, VAL))
        s = s + dot_t(krot[...], chunk[:, :, VAL:GRAD].reshape(SPAN, 128))
        lane = lax.broadcasted_iota(jnp.int32, (1, SPAN), 1)
        qpos = jnp.zeros((1, SPAN), jnp.int32)
        for k in range(NY):
            qpos = jnp.where(lane // HEADS == k, qpos_ref[zs * 2 * NY + 2 * k + c], qpos)
        key_pos = lax.broadcasted_iota(jnp.int32, (2 * KEYS, SPAN), 0) + mine * 2 * KEYS
        seen = (vis[...] > 0.5) & (key_pos <= qpos)
        s = jnp.where(seen, s * score_scale, -1e30)
        top = jnp.maximum(jnp.max(s, axis=0, keepdims=True), -1e20)
        p = jnp.exp(s - top)
        dp = dot_t(values, chunk[:, :, GRAD:BLOCK].reshape(SPAN, VAL))
        pbuf[zs] = p
        dbuf[zs] = dp
        stat[zs, 0:1] = top
        stat[zs, 1:2] = jnp.sum(p, axis=0, keepdims=True)
        stat[zs, 2:3] = jnp.sum(p * dp, axis=0, keepdims=True)
        stat[zs, 3:8] = jnp.zeros((5, SPAN), jnp.float32)

        @pl.when(zs != zl)
        def _():
            remote(
                stat.at[zs], stat_z.at[zl], z_send.at[0], z_recv.at[zl], at(zl=zs)
            ).start()

    def places(d, work):
        def body(k, _):
            zs = jnp.where(k == 0, zl + d, zl - d)
            pl.when((zs >= 0) & (zs < NZ))(lambda: work(zs))
            return 0

        if d == 0:
            work(zl)
        else:
            lax.fori_loop(0, 2, body, 0)

    def inject(zs):
        source = zs * NY + y
        wait_rows(source)
        send_rows(source, at(y=y_up))
        send_rows(source, at(y=y_down))

    def pass_on(e):
        def work(zs):
            even = lax.rem(zs, 2) == 0
            rising = zs * NY + lax.rem(y + NY - e, NY)
            falling = zs * NY + lax.rem(y + e, NY)
            if e <= 3:
                wait_rows(rising)
                if e < 3:
                    send_rows(rising, at(y=y_up))
                else:
                    pl.when(even)(lambda: send_rows(rising, at(y=y_up)))
                wait_rows(falling)
                if e < 3:
                    send_rows(falling, at(y=y_down))
                else:
                    pl.when(jnp.logical_not(even))(lambda: send_rows(falling, at(y=y_down)))
            else:
                wait_rows(rising)

        return work

    first = next(event for event in ORDER if event[0] == "c")
    for event in ORDER:
        kind, d = event[0], int(event[1])
        if kind == "z":
            places(d, inject)
        elif kind == "y":
            places(d, pass_on(int(event[2])))
        elif kind == "r":
            places(d, rest_relay)
        elif kind == "c":
            if event == first:
                take_keys()
            places(d, first_pass)
        else:
            for k in range(1, NY):
                block, send, recv = rest_along_y(lax.rem(y + k, NY))
                remote(block, block, send, recv, sibling).wait_recv()
            for half in range(2):
                rest_send(zl, half)

    def merged(parts):
        top = parts[0][0:1]
        for part in parts[1:]:
            top = jnp.maximum(top, part[0:1])
        total = jnp.zeros_like(top)
        weighted = jnp.zeros_like(top)
        for part in parts:
            gain = jnp.exp(part[0:1] - top)
            total = total + part[1:2] * gain
            weighted = weighted + part[2:3] * gain
        return top, total, weighted

    stat_z[zl] = stat[zl]
    for z in z_peers:
        remote(stat.at[0], stat_z.at[z], z_send.at[0], z_recv.at[z], sibling).wait_recv()
    top, total, weighted = merged([stat_z[k] for k in range(NZ)])
    stat_y[y, 0:1] = top
    stat_y[y, 1:2] = total
    stat_y[y, 2:3] = weighted
    stat_y[y, 3:8] = jnp.zeros((5, SPAN), jnp.float32)
    for d in range(1, NY):
        remote(
            stat_y.at[y], stat_y.at[y], y_send.at[0], y_recv.at[y], at(y=lax.rem(y + d, NY))
        ).start()
    for d in range(1, NY):
        k = lax.rem(y + d, NY)
        remote(stat_y.at[k], stat_y.at[k], y_send.at[0], y_recv.at[k], sibling).wait_recv()
    top, total, weighted = merged([stat_y[k] for k in range(NY)])
    stat_f[zl, 0:1] = top + jnp.log(total)
    stat_f[zl, 1:2] = weighted / total
    stat_f[zl, 2:8] = jnp.zeros((6, SPAN), jnp.float32)
    for z in z_peers:
        remote(stat_f.at[zl], stat_f.at[zl], f_send.at[0], f_recv.at[zl], at(zl=z)).start()

    def second_pass(zs):
        gain = jnp.exp(stat[zs, 0:1] - stat_f[zs, 0:1])
        p = pbuf[zs] * gain
        pb[zs] = p.astype(jnp.bfloat16)
        dsb[zs] = (p * (dbuf[zs] - stat_f[zs, 1:2])).astype(jnp.bfloat16)

    def each(k, _):
        zs = lax.rem(zl + k, NZ)

        @pl.when(k > 0)
        def _():
            remote(stat_f.at[zs], stat_f.at[zs], f_send.at[0], f_recv.at[zs], sibling).wait_recv()

        second_pass(zs)
        return 0

    lax.fori_loop(0, NZ, each, 0)

    def gradient(half, piece):
        first = pl.multiple_of(half * KEYS, KEYS)
        lo = piece * 256
        value = jnp.zeros((KEYS, 256), jnp.float32)
        key = jnp.zeros((KEYS, 256), jnp.float32)
        turn = jnp.zeros((KEYS, 128), jnp.float32)
        for k in range(NZ):
            chunk = rows.at[k * NY : (k + 1) * NY]
            ds_k = dsb[k, pl.ds(first, KEYS)]
            key = key + dot(ds_k, chunk[:, :, lo : lo + 256].reshape(SPAN, 256))
            value = value + dot(
                pb[k, pl.ds(first, KEYS)],
                chunk[:, :, GRAD + lo : GRAD + lo + 256].reshape(SPAN, 256),
            )
            if piece == 1:
                turn = turn + dot(ds_k, chunk[:, :, VAL:GRAD].reshape(SPAN, 128))
        both = (key * score_scale + value).reshape(NX, 64, 256)
        tiles = [both[:, :, 0:128], both[:, :, 128:256]]
        if piece == 1:
            turn = (turn * score_scale).reshape(NX, 2, 32, 128)
            lane = lax.broadcasted_iota(jnp.int32, (NX, 32, 128), 2)
            tiles.append(jnp.where(lane < 64, turn[:, 0], turn[:, 1]))
        return jnp.concatenate(tiles, axis=1)

    for piece, (lo, size) in enumerate(SPLIT):
        s1[:, lo : lo + size] = gradient(1 - c, piece).astype(jnp.bfloat16)
        part = pl.ds(lo, size)
        remote(
            s1.at[:, part], r1.at[:, part], r1_send.at[piece], r1_recv.at[piece], sibling
        ).start()
    for piece, (lo, size) in enumerate(SPLIT):
        own = gradient(c, piece)
        part = pl.ds(lo, size)
        remote(
            s1.at[:, part], r1.at[:, part], r1_send.at[piece], r1_recv.at[piece], sibling
        ).wait()
        s2[:, lo : lo + size] = (own + r1[:, lo : lo + size].astype(jnp.float32)).astype(
            jnp.bfloat16
        )
        for k in x_peers:
            remote(
                s2.at[k, part], r2.at[x, part], r2_send.at[piece], r2_recv.at[piece, x], at(x=k)
            ).start()
    for piece, (lo, size) in enumerate(SPLIT):
        part = pl.ds(lo, size)
        for k in x_peers:
            remote(
                s2.at[k, part], r2.at[k, part], r2_send.at[piece], r2_recv.at[piece, k], at(x=k)
            ).wait_recv()
        total = s2[x, lo : lo + size].astype(jnp.float32)
        for k in x_peers:
            total = total + r2[k, lo : lo + size].astype(jnp.float32)
        s3[lo : lo + size] = total.astype(jnp.bfloat16)
        remote(s3.at[part], r3.at[part], r3_send.at[piece], r3_recv.at[piece], across).start()
    for piece, (lo, size) in enumerate(SPLIT):
        part = pl.ds(lo, size)
        remote(s3.at[part], r3.at[part], r3_send.at[piece], r3_recv.at[piece], across).wait()
        total = s3[lo : lo + size].astype(jnp.float32) + r3[lo : lo + size].astype(jnp.float32)
        fin[x, lo : lo + size] = total.astype(jnp.bfloat16)
        for k in x_peers:
            remote(
                fin.at[x, part], fin.at[x, part], r4_send.at[piece], r4_recv.at[piece, x], at(x=k)
            ).start()
    for piece, (lo, size) in enumerate(SPLIT):
        part = pl.ds(lo, size)
        for k in x_peers:
            remote(
                fin.at[k, part], fin.at[k, part], r4_send.at[piece], r4_recv.at[piece, k], at(x=k)
            ).wait_recv()
    for k in range(NX):
        for tile in range(4):
            out_ref[k * 64 : (k + 1) * 64, tile * 128 : (tile + 1) * 128] = fin[
                k, tile * 64 : (tile + 1) * 64
            ]
        out_ref[k * 64 : k * 64 + 32, VAL:LAT] = fin[k, 256:288, 0:64]
        out_ref[k * 64 + 32 : (k + 1) * 64, VAL:LAT] = fin[k, 256:288, 64:128]

    for zs in range(NZ):
        rest_drain(zs)
    block, send, recv = rest_along_y(y)
    seven = rows.at[pl.ds(0, 7), :, pl.ds(CUT, BLOCK - CUT)]
    remote(seven, seven, send, recv, sibling).wait_send()
    most = rows.at[pl.ds(0, NZ * NY - 1), :, pl.ds(0, CUT)]
    remote(most, most, g_send.at[0], g_recv.at[0], sibling).wait_send()
    swap.wait_send()
    for buffer, sem in ((stat, z_send), (stat_y, y_send), (stat_f, f_send)):
        seven = buffer.at[pl.ds(0, 7)]
        remote(seven, seven, sem.at[0], z_recv.at[0], sibling).wait_send()
    for piece, (lo, size) in enumerate(SPLIT):
        three = s2.at[pl.ds(0, 3), pl.ds(lo, size)]
        remote(three, three, r2_send.at[piece], r2_recv.at[piece, 0], sibling).wait_send()
        remote(three, three, r4_send.at[piece], r4_recv.at[piece, 0], sibling).wait_send()


def latent_gradient(query_pos, valid_keys, queries, output_gradient, latents):
    bf16, f32 = jnp.bfloat16, jnp.float32
    vmem, smem = pl.BlockSpec(memory_space=pltpu.VMEM), pl.BlockSpec(memory_space=pltpu.SMEM)
    dma = pltpu.SemaphoreType.DMA
    return pl.pallas_call(
        kernel,
        out_shape=jax.ShapeDtypeStruct((KEYS, LAT), bf16),
        in_specs=[smem, smem, vmem, vmem, vmem],
        out_specs=vmem,
        scratch_shapes=[
            pltpu.VMEM((NZ * NY, HEADS, BLOCK), bf16),
            pltpu.VMEM((2, KEYS, 640), bf16),
            pltpu.VMEM((2 * KEYS, 128), bf16),
            pltpu.VMEM((2 * KEYS, 128), f32),
            pltpu.VMEM((NZ, 2 * KEYS, SPAN), f32),
            pltpu.VMEM((NZ, 2 * KEYS, SPAN), f32),
            pltpu.VMEM((NZ, 2 * KEYS, SPAN), bf16),
            pltpu.VMEM((NZ, 2 * KEYS, SPAN), bf16),
            pltpu.VMEM((NZ, 8, SPAN), f32),
            pltpu.VMEM((NZ, 8, SPAN), f32),
            pltpu.VMEM((NY, 8, SPAN), f32),
            pltpu.VMEM((NZ, 8, SPAN), f32),
            pltpu.VMEM((NX, PART, 128), bf16),
            pltpu.VMEM((NX, PART, 128), bf16),
            pltpu.VMEM((NX, PART, 128), bf16),
            pltpu.VMEM((NX, PART, 128), bf16),
            pltpu.VMEM((PART, 128), bf16),
            pltpu.VMEM((PART, 128), bf16),
            pltpu.VMEM((NX, PART, 128), bf16),
            dma((NZ * NY,)), dma((1,)), dma((NY,)), dma((1,)), dma((NZ, 2)), dma((NZ, 2, 2)),
            dma((1,)), dma((1,)),
            dma((NZ,)), dma((1,)), dma((NY,)), dma((1,)), dma((NZ,)), dma((1,)),
            dma((2,)), dma((2,)), dma((2, NX)), dma((2,)),
            dma((2,)), dma((2,)), dma((2, NX)), dma((2,)),
        ],
        compiler_params=pltpu.CompilerParams(
            collective_id=0, has_side_effects=True, vmem_limit_bytes=40 * 2**20
        ),
        cost_estimate=pl.CostEstimate(
            flops=2_500_000_000, bytes_accessed=1_000_000, transcendentals=600_000
        ),
    )(query_pos, valid_keys, queries, output_gradient, latents)


def shards(queries, query_pos, latents, valid_keys, output_gradient, kv_down):
    latent_b = latent_gradient(query_pos, valid_keys, queries, output_gradient, latents)
    input_grad = lax.dot_general(
        latent_b, kv_down, (((1,), (1,)), ((), ())), preferred_element_type=jnp.float32
    ).astype(jnp.bfloat16)
    return (latent_b.astype(jnp.float32), input_grad)


def solution(mesh):
    torus = Mesh(mesh.devices.reshape(NX, 2, NZ, NY, 2), AXES)
    placed = (
        P(SEQ, HEAD, None),
        P(),
        P(SEQ, None),
        P(SEQ),
        P(SEQ, HEAD, None),
        P(HEAD, None),
    )
    return jax.shard_map(
        shards,
        mesh=torus,
        in_specs=placed,
        out_specs=(P(SEQ, None), P(SEQ, HEAD)),
        check_vma=False,
    )
```
